32 devices in a mesh: rep: 8 (over y, x, core), tp: 4 (over z).
Axes of the slice: x: 2, y: 2, z: 4, core: 2. Of those that a mesh axis runs over, the one named last changes fastest.
Arguments:
- hidden: bfloat16 [4096, 8192], P('rep'), may hold values from -36 to 36
- segment_ids: int32 [8, 512], P('rep'), may hold values from 0 to 3, never falling along the last dimension, each value on 1 to 256 neighbouring positions
- norm_gain: bfloat16 [8192], replicated, may hold values from 0.5 to 2
- qkv_weight: bfloat16 [8192, 10240], P(('rep', 'tp')), may hold values from -2 to 2
- qkv_bias: bfloat16 [10240], replicated, may hold values from -13 to 13
Outputs:
- attended: bfloat16 [4096, 8192], P('rep', 'tp')
- block_peak: bfloat16 [64, 80], P(None, 'tp')
The draws below stay inside these ranges and needn't reach their ends.
All inputs are finite; a program needn't handle non-finite values.
Results may differ from the reference program's by a relative error of at most 0.007.
The reference program's roundings to bfloat16 on the way count: a program that leaves them out, or rounds other values in their place, can miss the bound.
Values may be sent and summed in bfloat16 or wider, within the bound.
No kernel may reach another device: no remote copies, remote signals or barrier semaphores. Data moves between devices by JAX's collectives and lax.ppermute only.
A program may use at most 512 MiB of HBM per device.

```python
import math
import jax
import jax.numpy as jnp
import numpy as np
from jax import lax

D = 8192
HEADS = 64
KV = 8
HD = 128
BLOCK = 128
TOK = 512
REPS = 8
QKV = 10240


def log_spread(key, shape, low_value, high_value):
    return jnp.exp(jax.random.uniform(key, shape, jnp.float32, math.log(low_value), math.log(high_value)))


def draw_hidden(key, part):
    key = jax.random.fold_in(key, 1)
    key_base, key_rows, key_cols = jax.random.split(key, 3)
    row_scale = log_spread(key_rows, (REPS * TOK, 1), 0.3, 3.0)
    col_scale = log_spread(key_cols, (1, D), 0.3, 3.0)
    base = jax.random.truncated_normal(key_base, -4.0, 4.0, (REPS * TOK, D), jnp.float32)
    return (base * row_scale * col_scale).astype(jnp.bfloat16)


def draw_qkv_weight(key, part):
    key = jax.random.fold_in(key, 2)
    key_base, key_rows, key_cols = jax.random.split(key, 3)
    row_scale = log_spread(key_rows, (D, 1), 0.35, 2.8)
    col_scale = log_spread(key_cols, (1, QKV), 0.5, 2.0)
    base = jax.random.truncated_normal(key_base, -4.0, 4.0, (D, QKV), jnp.float32)
    return (base * row_scale * col_scale * D ** (-0.5)).astype(jnp.bfloat16)


def draw_qkv_bias(key, part):
    key = jax.random.fold_in(key, 3)
    key_noise = jax.random.fold_in(key, 0)
    base = jax.random.truncated_normal(key_noise, -4.0, 4.0, (QKV,), jnp.float32)
    return (0.5 * base).astype(jnp.bfloat16)


def profile(amount, total, limit, skew):
    portions = [(1 << 20) // math.isqrt(grade ** skew) + 1 for grade in range(2, amount + 1)]
    rest, holding = total - limit - (amount - 1), [1] * (amount - 1)
    while rest > 0:
        candidates = [i for i in range(amount - 1) if holding[i] < limit]
        pool, budget = sum([portions[i] for i in candidates]), rest
        for i in candidates:
            addition = min(limit - holding[i], max(1, budget * portions[i] // pool), rest)
            holding[i] = holding[i] + addition
            rest = rest - addition
    return np.array([limit] + holding)


def ragged(own_key, amount, total, limit, lean):
    if amount == 2:
        one = jax.random.randint(own_key, (), max(1, total - limit), min(limit, total - 1) + 1)
        return jnp.stack([one, total - one])
    tallies = jnp.asarray(profile(amount, total, limit, lean), jnp.int32)
    couples = (amount - 1) // 2
    donor, receiver = tallies[1:1 + 2 * couples:2], tallies[2:2 + 2 * couples:2]
    room = jnp.minimum(donor - 1, limit - receiver)
    shifted = jax.random.randint(jax.random.fold_in(own_key, 1), (couples,), 0, 1 << 20) % (room + 1)
    tallies = tallies.at[1:1 + 2 * couples:2].set(donor - shifted).at[2:2 + 2 * couples:2].set(receiver + shifted)
    return tallies[jax.random.permutation(jax.random.fold_in(own_key, 2), amount)]


def setup_inputs(seed: int = 0) -> dict:
    streams_of = jax.random.split(jax.random.key(seed), 6)
    hidden = draw_hidden(jax.random.fold_in(streams_of[5], 71), 0)
    segment_ids = jax.vmap(lambda own: jnp.searchsorted(jnp.cumsum(ragged(own, max(3, TOK // 128), TOK, TOK // 2, 1)), jnp.arange(TOK), side="right"))(jax.random.split(streams_of[1], REPS)).reshape((REPS, TOK)).astype(jnp.int32)
    norm_gain = jnp.clip(jnp.exp(jax.random.uniform(streams_of[2], (D,), jnp.float32, math.log(0.5), math.log(2.0))), 0.5, 2.0).astype(jnp.bfloat16)
    qkv_weight = draw_qkv_weight(jax.random.fold_in(streams_of[5], 71), 0)
    qkv_bias = draw_qkv_bias(jax.random.fold_in(streams_of[5], 71), 0)
    return {"hidden": hidden, "segment_ids": segment_ids, "norm_gain": norm_gain, "qkv_weight": qkv_weight, "qkv_bias": qkv_bias}


theta_base = 1000000.0
code_limit = 448.0

def coarse_code(scaled):
    magnitude = jnp.abs(scaled)
    step_size = jnp.full_like(magnitude, 2.0 ** (-9))
    for exponent in range(-5, 9):
        step_size = jnp.where(magnitude >= 2.0 ** exponent, 2.0 ** (exponent - 3), step_size)
    return jnp.sign(scaled) * jnp.floor(magnitude / step_size + 0.5) * step_size

def tile_peaks(weight, row_block, col_block):
    row_count, col_count = weight.shape
    tile_view = jnp.abs(weight).reshape(row_count // row_block, row_block, col_count // col_block, col_block)
    return lax.optimization_barrier(jnp.max(tile_view, axis=(1, 3)))

def tile_scales(peak_tiles):
    return (peak_tiles.astype(jnp.float32) + 1e-06) / code_limit

def encode(weight, peak_tiles, row_block, col_block):
    row_count, col_count = weight.shape
    tile_view = weight.astype(jnp.float32).reshape(row_count // row_block, row_block, col_count // col_block, col_block)
    scaled = tile_view / tile_scales(peak_tiles)[:, None, :, None]
    return coarse_code(scaled).astype(jnp.bfloat16).reshape(row_count, col_count)

def decode(code_tiles, peak_tiles, block_side):
    row_count, col_count = code_tiles.shape
    tile_view = code_tiles.astype(jnp.float32).reshape(row_count // block_side, block_side, col_count // block_side, block_side)
    scaled = tile_view * tile_scales(peak_tiles)[:, None, :, None]
    return scaled.astype(jnp.bfloat16).reshape(row_count, col_count)

def rms_norm(hidden_rows, norm_gain):
    values_f = hidden_rows.astype(jnp.float32)
    inverse = lax.rsqrt(lax.optimization_barrier(jnp.mean(values_f * values_f, axis=-1, keepdims=True)) + 1e-06)
    return (values_f * inverse * norm_gain.astype(jnp.float32)).astype(jnp.bfloat16)

def token_positions(segments):
    token_index = jnp.arange(segments.shape[0], dtype=jnp.int32)
    same_doc = (segments[:, None] == segments[None, :]) & (token_index[None, :] < token_index[:, None])
    return lax.optimization_barrier(jnp.sum(same_doc.astype(jnp.int32), axis=1))

def rotary(head_values, position):
    half_width = head_values.shape[-1] // 2
    freq_index = jnp.arange(half_width, dtype=jnp.float32)
    frequency = jnp.exp(freq_index * (-2.0 / head_values.shape[-1]) * math.log(theta_base))
    angles = position.astype(jnp.float32)[:, None] * frequency[None, :]
    shape_out = (head_values.shape[0],) + (1,) * (head_values.ndim - 2) + (half_width,)
    cosine = jnp.cos(angles).reshape(shape_out)
    sine_part = jnp.sin(angles).reshape(shape_out)
    front_half = head_values[..., :half_width]
    back_half = head_values[..., half_width:]
    return jnp.concatenate([front_half * cosine - back_half * sine_part, back_half * cosine + front_half * sine_part], axis=-1)

def split_heads(projected, position):
    per_head = HEADS // KV
    token_total = projected.shape[0]
    groups = projected.shape[1] // ((per_head + 2) * HD)
    grouped = projected.reshape(token_total, groups, per_head + 2, HD)
    query_heads = rotary(grouped[:, :, :per_head, :], position).astype(jnp.bfloat16)
    key_heads = rotary(grouped[:, :, per_head, :], position).astype(jnp.bfloat16)
    value_heads = grouped[:, :, per_head + 1, :].astype(jnp.bfloat16)
    return (query_heads, key_heads, value_heads)

def attend(query_heads, key_heads, value_heads, segments, block_rows):
    token_total = query_heads.shape[0]
    token_index = jnp.arange(token_total, dtype=jnp.int32)
    scale_factor = 1.0 / math.sqrt(query_heads.shape[-1])

    def one_block(first_row):
        query_part = lax.dynamic_slice_in_dim(query_heads, first_row, block_rows, 0)
        row_ids = first_row + jnp.arange(block_rows, dtype=jnp.int32)
        row_segments = lax.dynamic_slice_in_dim(segments, first_row, block_rows, 0)
        allowed = (row_segments[:, None] == segments[None, :]) & (token_index[None, :] <= row_ids[:, None])
        scores = jnp.einsum('tgqd,sgd->gqts', query_part.astype(jnp.float32), key_heads.astype(jnp.float32)) * scale_factor
        scores = jnp.where(allowed, scores, -1e+30)
        row_max = lax.optimization_barrier(jnp.max(scores, axis=-1, keepdims=True))
        weights_raw = jnp.where(allowed, jnp.exp(scores - row_max), 0.0)
        probabilities = (weights_raw / lax.optimization_barrier(jnp.sum(weights_raw, axis=-1, keepdims=True))).astype(jnp.bfloat16)
        mixed_out = jnp.einsum('gqts,sgd->tgqd', probabilities.astype(jnp.float32), value_heads.astype(jnp.float32))
        return mixed_out.astype(jnp.bfloat16)
    starts = jnp.arange(token_total // block_rows, dtype=jnp.int32) * block_rows
    pieces = lax.map(one_block, starts)
    return pieces.reshape(token_total, -1)

def reference(hidden, segment_ids, norm_gain, qkv_weight, qkv_bias):
    peak_tiles = tile_peaks(qkv_weight, BLOCK, BLOCK)
    code_tiles = encode(qkv_weight, peak_tiles, BLOCK, BLOCK)
    restored = decode(code_tiles, peak_tiles, BLOCK)
    block_rows = min(512, TOK)

    def one_replica(replica):
        hidden_rows = lax.dynamic_slice_in_dim(hidden, replica * TOK, TOK, 0)
        segments = lax.dynamic_index_in_dim(segment_ids, replica, 0, keepdims=False)
        normed = rms_norm(hidden_rows, norm_gain)
        projected = jnp.dot(normed, restored, preferred_element_type=jnp.float32) + qkv_bias.astype(jnp.float32)
        query_heads, key_heads, value_heads = split_heads(projected, token_positions(segments))
        return attend(query_heads, key_heads, value_heads, segments, block_rows)
    outputs = lax.map(one_replica, jnp.arange(REPS, dtype=jnp.int32))
    return (outputs.reshape(REPS * TOK, HEADS * HD), peak_tiles)
```

```python
import functools
import math

import jax
import jax.numpy as jnp
import numpy as np
from jax import lax
from jax.experimental import pallas as pl
from jax.experimental.pallas import tpu as pltpu
from jax.sharding import PartitionSpec as P

HEADS = 64
KV = 8
HD = 128
BLOCK = 128
UNIT = 2 * HD
PER_GROUP = (HEADS // KV + 2) * HD // UNIT

theta_base = 1000000.0
code_limit = 448.0
KERNEL_VMEM = 30 * 2**20


def after(value, *others):
    others = tuple(o for o in others if o is not None)
    return lax.optimization_barrier((value,) + others)[0] if others else value


def tile_scale(peak):
    return (peak + 1e-06) / code_limit


def tile_factor(scale):
    return (1.0 / scale) * (1.0 + 1.75e-07)


def restored_tile(tile, scale, factor):
    scaled = tile * factor
    lean = jnp.abs(scaled) * 0.750001
    wide = lean * (2.0**23 + 1.0)
    power = wide - (wide - lean)
    anchor = jnp.maximum(power * (1.5 * 2.0**20), 1.5 * 2.0**14)
    codes = (scaled + anchor) - anchor
    return codes * scale


def restore_kernel(views, table, *refs):
    count = len(refs) // (views + 1)
    sources, targets = refs[: count * views], refs[count * views :]
    tiles = []
    for n, source in enumerate(sources):
        target, shift = targets[n // views], n % views * UNIT
        for row in range(0, source.shape[0], BLOCK):
            for col in range(0, UNIT, BLOCK):
                here = (slice(row, row + BLOCK), slice(col, col + BLOCK))
                there = (here[0], slice(shift + col, shift + col + BLOCK))
                tiles.append((source, here, target, there))
    scales = []
    for source, here, _, _ in tiles:
        peak = jnp.max(jnp.abs(source[here]), axis=0, keepdims=True).astype(jnp.float32)
        scales.append(tile_scale(jnp.max(peak, axis=1, keepdims=True)))
    factors = [tile_factor(scale) for scale in scales]
    for (source, here, target, there), scale, factor in zip(tiles, scales, factors):
        tile = source[here].astype(jnp.float32)
        target[there] = restored_tile(tile, scale, factor).astype(target.dtype)


def restore(weight, table):
    rows = weight.shape[0]
    count, steps = table.shape
    views = 2 if count == 1 and steps % 2 == 0 else 1
    spec_in = [
        pl.BlockSpec(
            (rows, UNIT), functools.partial(lambda o, v, i, tab: (0, tab[o, i * views + v]), o, v)
        )
        for o in range(count)
        for v in range(views)
    ]
    return pl.pallas_call(
        functools.partial(restore_kernel, views),
        grid_spec=pltpu.PrefetchScalarGridSpec(
            num_scalar_prefetch=1,
            grid=(steps // views,),
            in_specs=spec_in,
            out_specs=[pl.BlockSpec((rows, views * UNIT), lambda i, tab: (0, i))] * count,
        ),
        out_shape=[jax.ShapeDtypeStruct((rows, steps * UNIT), weight.dtype)] * count,
        compiler_params=pltpu.CompilerParams(vmem_limit_bytes=KERNEL_VMEM),
        cost_estimate=pl.CostEstimate(
            flops=16 * rows * UNIT * steps * count,
            bytes_accessed=4 * rows * UNIT * steps * count,
            transcendentals=0,
        ),
    )(table, *([weight] * (count * views)))


def peaks_kernel(weight, fence, out):
    lanes = lax.broadcasted_iota(jnp.int32, out.shape, 1)
    sub = lax.broadcasted_iota(jnp.int32, out.shape, 0)

    def step(j, held):
        cols = pl.ds(pl.multiple_of(j * BLOCK, BLOCK), BLOCK)
        for row in range(weight.shape[0] // BLOCK):
            tile = jnp.abs(weight[row * BLOCK : (row + 1) * BLOCK, cols])
            peak = jnp.max(tile, axis=0, keepdims=True).astype(jnp.float32)
            peak = jnp.max(peak, axis=1, keepdims=True)
            held = jnp.where((lanes == j) & (sub == row), peak, held)
        return held

    out[...] = lax.fori_loop(
        0, weight.shape[1] // BLOCK, step, jnp.zeros(out.shape, jnp.float32), unroll=8
    )


def tile_peaks(weight, *others):
    rows, cols = weight.shape
    if rows % BLOCK == 0 and cols // BLOCK <= 128 and rows // BLOCK <= 8:
        held = pl.pallas_call(
            peaks_kernel,
            in_specs=[
                pl.BlockSpec((rows, cols), lambda: (0, 0)),
                pl.BlockSpec(memory_space=pltpu.SMEM),
            ],
            out_shape=jax.ShapeDtypeStruct((8, 128), jnp.float32),
            compiler_params=pltpu.CompilerParams(vmem_limit_bytes=KERNEL_VMEM),
            cost_estimate=pl.CostEstimate(
                flops=2 * rows * cols, bytes_accessed=2 * rows * cols, transcendentals=0
            ),
        )(weight, after(jnp.zeros((1,), jnp.int32), *others))
        return held[: rows // BLOCK, : cols // BLOCK].astype(weight.dtype)
    block = min(BLOCK, rows)
    view = jnp.abs(weight).reshape(rows // block, block, cols // BLOCK, BLOCK)
    return jnp.max(view, axis=(1, 3))


def shared_peaks(weight, shared):
    peaks = tile_peaks(weight)
    for bit in range(shared.bit_length() - 1):
        pairs = [(s, s ^ 2**bit) for s in range(lax.axis_size("tp"))]
        peaks = jnp.maximum(peaks, lax.ppermute(peaks, "tp", pairs))
    return peaks


def restore_plain(weight, peaks):
    rows, cols = weight.shape
    view = weight.astype(jnp.float32).reshape(
        peaks.shape[0], rows // peaks.shape[0], cols // BLOCK, BLOCK
    )
    scale = tile_scale(peaks.astype(jnp.float32)[:, None, :, None])
    held = restored_tile(view, scale, tile_factor(scale))
    return held.astype(weight.dtype).reshape(rows, cols)


def norm_kernel(block, table, hidden, gain, *outs):
    values = hidden[...].astype(jnp.float32)
    mean = jnp.sum(values * values, axis=-1, keepdims=True) * (1.0 / values.shape[1])
    inverse = lax.rsqrt(mean + 1e-06)
    for o, out in enumerate(outs):
        for b in range(out.shape[1] // block):
            cols = pl.ds(pl.multiple_of(table[o, b] * block, block), block)
            part = hidden[:, cols].astype(jnp.float32) * inverse * gain[:, cols]
            out[:, b * block : (b + 1) * block] = part.astype(out.dtype)


def norm(hidden, gain, table, block):
    tokens, depth = hidden.shape
    count, blocks = table.shape
    if block % 128 == 0:
        rows = min(64, tokens)
        return pl.pallas_call(
            functools.partial(norm_kernel, block),
            grid_spec=pltpu.PrefetchScalarGridSpec(
                num_scalar_prefetch=1,
                grid=(tokens // rows,),
                in_specs=[
                    pl.BlockSpec((rows, depth), lambda i, tab: (i, 0)),
                    pl.BlockSpec((1, depth), lambda i, tab: (0, 0)),
                ],
                out_specs=[pl.BlockSpec((rows, blocks * block), lambda i, tab: (i, 0))] * count,
            ),
            out_shape=[jax.ShapeDtypeStruct((tokens, blocks * block), hidden.dtype)] * count,
            compiler_params=pltpu.CompilerParams(vmem_limit_bytes=KERNEL_VMEM),
            cost_estimate=pl.CostEstimate(
                flops=6 * tokens * depth, bytes_accessed=4 * tokens * depth, transcendentals=0
            ),
        )(table, hidden, gain.astype(jnp.float32).reshape(1, depth))
    values = hidden.astype(jnp.float32)
    inverse = lax.rsqrt(jnp.mean(values * values, axis=-1, keepdims=True) + 1e-06)
    normed = (values * inverse * gain.astype(jnp.float32)).astype(hidden.dtype)
    view = normed.reshape(tokens, depth // block, block)
    return [jnp.take(view, table[o], axis=1).reshape(tokens, blocks * block) for o in range(count)]


def product_kernel(offsets, runs, n_x, n_acc, *refs):
    xs, refs = refs[: n_x * runs], refs[n_x * runs :]
    pieces, refs = refs[: len(offsets)], refs[len(offsets) :]
    accs, refs = refs[:n_acc], refs[n_acc:]
    outs, (x_held, w_held, x_sems, w_sems) = refs[:n_x], refs[n_x:]
    height, width = pieces[0].shape[0], outs[0].shape[1]
    group = len(pieces) // runs
    copies = []
    for r in range(runs):
        own = [
            pltpu.make_async_copy(xs[n * runs + r], x_held.at[n, r], x_sems.at[n, r])
            for n in range(n_x)
        ]
        for p in range(r * group, (r + 1) * group):
            own.append(
                pltpu.make_async_copy(
                    pieces[p].at[:, pl.ds(offsets[p], width)],
                    w_held.at[r, pl.ds((p - r * group) * height, height), :],
                    w_sems.at[p],
                )
            )
        copies.append(own)
        for copy in own:
            copy.start()
    for r in range(runs):
        for copy in copies[r]:
            copy.wait()
        for n, out in enumerate(outs):
            part = jnp.dot(x_held[n, r], w_held[r], preferred_element_type=jnp.float32)
            if r > 0:
                part = out[...] + part
            elif n_acc:
                part = accs[n][...] + part
            out[...] = part


def product(xs, pieces, offsets, width, accs=()):
    runs = len(xs[0])
    tokens, depth = xs[0][0].shape
    if pieces[0].shape[0] % 128:
        held = jnp.concatenate([p[:, o : o + width] for p, o in zip(pieces, offsets)], axis=0)
        outs = [
            jnp.dot(jnp.concatenate(x, axis=1), held, preferred_element_type=jnp.float32) for x in xs
        ]
        return [a + o for a, o in zip(accs, outs)] if accs else outs
    count = len(xs)
    return pl.pallas_call(
        functools.partial(product_kernel, tuple(offsets), runs, count, len(accs)),
        in_specs=[pl.BlockSpec(memory_space=pl.ANY)] * (count * runs + len(pieces))
        + [pl.BlockSpec(memory_space=pltpu.VMEM)] * len(accs),
        out_specs=[pl.BlockSpec(memory_space=pltpu.VMEM)] * count,
        out_shape=[jax.ShapeDtypeStruct((tokens, width), jnp.float32)] * count,
        scratch_shapes=[
            pltpu.VMEM((count, runs, tokens, depth), pieces[0].dtype),
            pltpu.VMEM((runs, depth, width), pieces[0].dtype),
            pltpu.SemaphoreType.DMA((count, runs)),
            pltpu.SemaphoreType.DMA((len(pieces),)),
        ],
        compiler_params=pltpu.CompilerParams(vmem_limit_bytes=KERNEL_VMEM),
        cost_estimate=pl.CostEstimate(
            flops=2 * count * tokens * runs * depth * width,
            bytes_accessed=2 * runs * depth * (count * tokens + width) + 4 * count * tokens * width,
            transcendentals=0,
        ),
    )(*[part for x in xs for part in x], *pieces, *accs)


def token_positions(segments):
    index = jnp.arange(segments.shape[0], dtype=jnp.int32)
    same = (segments[:, None] == segments[None, :]) & (index[None, :] < index[:, None])
    return jnp.sum(same.astype(jnp.int32), axis=1)


def rotary_tables(position):
    half = HD // 2
    index = jnp.arange(half, dtype=jnp.float32)
    frequency = jnp.exp(index * (-2.0 / HD) * math.log(theta_base))
    angles = position.astype(jnp.float32)[:, None] * frequency[None, :]
    cosine, sine = jnp.cos(angles), jnp.sin(angles)
    return (
        jnp.concatenate([cosine, cosine], axis=1),
        jnp.concatenate([-sine, sine], axis=1),
    )


def rotate(head, cosine, sine):
    return head * cosine + pltpu.roll(head, HD // 2, 1) * sine


def key_value_kernel(table, own, other, bias, cosine, sine, key, value):
    both = own[...] + other[...] + bias[...]
    key[...] = rotate(both[:, :HD], cosine[...], sine[...]).astype(key.dtype)
    value[...] = both[:, HD:].astype(value.dtype)


def key_value(own, other, bias, cosine, sine, table, dtype):
    tokens = own.shape[0]
    groups = table.shape[0]
    half = pl.BlockSpec((tokens, UNIT), lambda i, tab: (0, i))
    whole = pl.BlockSpec((tokens, HD), lambda i, tab: (0, 0))
    head = pl.BlockSpec((tokens, HD), lambda i, tab: (0, i))
    return pl.pallas_call(
        key_value_kernel,
        grid_spec=pltpu.PrefetchScalarGridSpec(
            num_scalar_prefetch=1,
            grid=(groups,),
            in_specs=[half, half, pl.BlockSpec((1, UNIT), lambda i, tab: (0, tab[i])), whole, whole],
            out_specs=[head, head],
        ),
        out_shape=[jax.ShapeDtypeStruct((tokens, groups * HD), dtype)] * 2,
        compiler_params=pltpu.CompilerParams(vmem_limit_bytes=KERNEL_VMEM),
        cost_estimate=pl.CostEstimate(
            flops=6 * tokens * groups * UNIT, bytes_accessed=10 * tokens * groups * UNIT, transcendentals=0
        ),
    )(table, own, other, bias, cosine, sine)


def attention_kernel(views, table, own, other, *refs):
    biases, (cosine, sine, key, value, seg_rows, seg_cols, _, out) = refs[:views], refs[views:]
    tokens = own.shape[0]
    rows = min(128, tokens)
    scale = math.log2(math.e) / math.sqrt(HD)
    queries = []
    for h in range(own.shape[1] // HD):
        cols = slice(h * HD, (h + 1) * HD)
        bias = biases[h * HD // UNIT][:, h * HD % UNIT : h * HD % UNIT + HD]
        query = own[:, cols] + other[:, cols] + bias
        queries.append(rotate(query, cosine[...], sine[...]).astype(key.dtype))
    count = len(queries)
    for first in range(0, tokens, rows):
        low, high = max(0, first - 256), first + rows
        row = first + lax.broadcasted_iota(jnp.int32, (rows, high - low), 0)
        col = low + lax.broadcasted_iota(jnp.int32, (rows, high - low), 1)
        allowed = (seg_rows[first:high, :] == seg_cols[:, low:high]) & (col <= row)
        scores = lax.dot_general(
            jnp.concatenate([query[first:high, :] for query in queries], axis=0),
            key[low:high, :],
            (((1,), (1,)), ((), ())),
            preferred_element_type=jnp.float32,
        )
        scores = jnp.where(allowed[None], scores.reshape(count, rows, high - low), -1e30)
        weights = jnp.exp2((scores - jnp.max(scores, axis=-1, keepdims=True)) * scale)
        total = jnp.sum(weights, axis=-1, keepdims=True)
        chances = (weights * (1.0 / total)).astype(value.dtype)
        mixed = jnp.dot(
            chances.reshape(count * rows, high - low),
            value[low:high, :],
            preferred_element_type=jnp.float32,
        ).astype(out.dtype)
        for h in range(count):
            out[first:high, h * HD : (h + 1) * HD] = mixed[h * rows : (h + 1) * rows]


def attention(own, other, bias, cosine, sine, key, value, segments, held, table, skip, base, width):
    tokens = own.shape[0]
    count = table.shape[0]
    per_group = HEADS // KV * HD // UNIT
    views = 2 if count % 2 == skip % 2 == base % 2 == 0 else 1
    half = pl.BlockSpec((tokens, views * UNIT), lambda i, tab: (0, skip // views + i))
    whole = pl.BlockSpec((tokens, HD), lambda i, tab: (0, 0))
    head = pl.BlockSpec((tokens, HD), lambda i, tab: (0, (base + i * views) // per_group))
    in_specs = [
        half,
        half,
        *[
            pl.BlockSpec((1, UNIT), functools.partial(lambda v, i, tab: (0, tab[i * views + v]), v))
            for v in range(views)
        ],
        whole,
        whole,
        head,
        head,
        pl.BlockSpec((tokens, 1), lambda i, tab: (0, 0)),
        pl.BlockSpec((1, tokens), lambda i, tab: (0, 0)),
    ]
    args = [table, own, other, *[bias] * views, cosine, sine, key, value]
    args += [segments[:, None], segments[None, :]]
    aliases = {}
    body = functools.partial(attention_kernel, views)
    if held is None:
        body = lambda *refs: attention_kernel(views, *refs[:-1], None, refs[-1])
    else:
        in_specs.append(pl.BlockSpec(memory_space=pl.ANY))
        args.append(held)
        aliases = {len(args) - 1: 0}
    return pl.pallas_call(
        body,
        grid_spec=pltpu.PrefetchScalarGridSpec(
            num_scalar_prefetch=1,
            grid=(count // views,),
            in_specs=in_specs,
            out_specs=pl.BlockSpec((tokens, views * UNIT), lambda i, tab: (0, base // views + i)),
        ),
        out_shape=jax.ShapeDtypeStruct((tokens, width), key.dtype),
        input_output_aliases=aliases,
        compiler_params=pltpu.CompilerParams(vmem_limit_bytes=KERNEL_VMEM),
        cost_estimate=pl.CostEstimate(
            flops=4 * tokens * tokens * UNIT * count,
            bytes_accessed=8 * tokens * UNIT * count,
            transcendentals=tokens * tokens * 2 * count,
        ),
    )(*args)


def peaks_here(weight, peaks, shared, *others):
    n_rep, n_tp = lax.axis_size("rep"), lax.axis_size("tp")
    rep, tp = lax.axis_index("rep"), lax.axis_index("tp")
    if peaks is None:
        peaks = tile_peaks(weight, *others)
    tiles = peaks.shape[1]
    for name, size, index in (("tp", n_tp, tp), ("rep", n_rep, rep)):
        for bit in range(size.bit_length() - 1):
            pairs = [(d, d ^ 2**bit) for d in range(size)]
            got = lax.ppermute(peaks, name, pairs)
            behind = (index >> bit) % 2 == 1
            first, second = jnp.where(behind, got, peaks), jnp.where(behind, peaks, got)
            peaks = jnp.concatenate([first, second], axis=0)
    return lax.dynamic_slice_in_dim(peaks, tp * (tiles // n_tp), tiles // n_tp, 1)[::shared]


def shards(hidden, segment_ids, norm_gain, qkv_weight, qkv_bias):
    n_rep, n_tp = lax.axis_size("rep"), lax.axis_size("tp")
    rep, tp = lax.axis_index("rep"), lax.axis_index("tp")
    rows, full_width = qkv_weight.shape
    shared = max(1, BLOCK // rows)
    groups = KV // n_tp
    local_units = groups * PER_GROUP
    dtype = qkv_weight.dtype

    bits = [2**b for b in range(1, n_rep.bit_length() - 1)]
    n_pieces = 2 ** len(bits)
    core = rep % 2

    def bit_of(step, of_core):
        return bits[(of_core + step) % len(bits)]

    def gather_step(value, step):
        return lax.ppermute(value, "rep", [(r, r ^ bit_of(step, r % 2)) for r in range(n_rep)])

    def to_core(value):
        return lax.ppermute(value, "rep", [(r, r ^ 1) for r in range(n_rep)])

    def to_server(value, shift):
        return lax.ppermute(value, "tp", [(t, (t + shift) % n_tp) for t in range(n_tp)])

    value_units = [g * PER_GROUP + PER_GROUP - 1 for g in range(groups)]
    query_units = [u for u in range(local_units) if u not in value_units]
    order = np.array(value_units + query_units, np.int32)
    counts = [2 * groups, 2 * groups, groups]
    starts = [0, counts[0], counts[0] + counts[1]]

    if shared == 1 and rows % BLOCK == 0:
        peaks = None

        def restored_units(shifts, first, count, *others):
            units = jnp.asarray(order[first : first + count])
            servers = (tp + jnp.asarray(shifts, jnp.int32)) % n_tp
            table = servers[:, None] * local_units + units[None, :]
            return restore(qkv_weight, after(table, *others))

    else:
        peaks = shared_peaks(qkv_weight, shared)
        plain = restore_plain(qkv_weight, peaks).reshape(rows, n_tp, local_units, UNIT)

        def restored_units(shifts, first, count, *others):
            out = []
            for shift in shifts:
                part = lax.dynamic_index_in_dim(plain, (tp + shift) % n_tp, 1, keepdims=False)
                out.append(part[:, order[first : first + count]].reshape(rows, count * UNIT))
            return out

    far = list(range(1, n_tp))
    n_far = len(far)
    own_a = restored_units([0], 0, counts[0])[0]
    far_units = restored_units(far, 0, counts[0]) if far else []
    step_masks = range(n_pieces)
    relative = np.zeros((2, n_pieces), np.int32)
    for k in range(2):
        for m in step_masks:
            for s in range(len(bits)):
                if m >> s & 1:
                    relative[k, m] ^= bit_of(s, k)
    relative = jnp.asarray(relative)
    shifts = jnp.arange(n_tp, dtype=jnp.int32)

    def depth_blocks(of_rep):
        source = of_rep ^ relative[of_rep % 2]
        server = (tp - shifts) % n_tp
        return (source[None, :] * n_tp + server[:, None]).reshape(-1)

    table = jnp.concatenate(
        [depth_blocks(r).reshape(n_tp, n_pieces) for r in (rep, rep ^ 1)], axis=0
    )
    pieces = []
    served = {}
    fences = {}
    n_units = 2 + 3 * n_far

    def arrived(u):
        return () if u < 0 else tuple(pieces[u][1:-1]) + (tuple(pieces[u - 1][-1:]) if u > 0 else ())

    def near(u):
        return pieces[u][min(1, n_pieces - 1)]

    def serve(u, held):
        fence = (near(u - 4),) if u >= 4 else ()
        served[u] = to_server(after(held, *fence), far[(u - 2) % n_far])

    def gather(held):
        u = len(pieces)
        got = [after(held, *arrived(u - 2), *fences.get(u, ()))]
        for step in range(len(bits)):
            got += [gather_step(g, step) for g in got]
        pieces.append(got)

    gather(own_a)
    for u in range(2, 2 + min(n_far, 3)):
        serve(u, far_units[u - 2])
    own_b = restored_units([0], counts[0], counts[1] + counts[2])[0]
    gather(own_b)
    far_units += restored_units(far, starts[1], counts[1])
    far_units += restored_units(far, starts[2], counts[2])
    parts = norm(hidden, norm_gain, table, rows)
    tokens = [[to_core(p) for p in parts[n_tp:]], parts[:n_tp]]
    segments = segment_ids[0]
    cosine, sine = rotary_tables(token_positions(segments))
    bias = qkv_bias.astype(jnp.float32).reshape(1, full_width)
    held = key = value = None
    base = 0
    for c in range(3):
        width = counts[c] * UNIT
        offset = (starts[c] - starts[min(c, 1)]) * UNIT
        columns = tp * local_units + jnp.asarray(order[starts[c] : starts[c] + counts[c]])
        for n in range(n_far):
            u = len(pieces)
            if u not in served:
                serve(u, far_units[u - 2])
            gather(served[u])
        chunk = [p for got in pieces[2 + c * n_far :] for p in got]
        both = pieces[min(c, 1)] + chunk
        offsets = [offset] * n_pieces + [0] * len(chunk)
        if c < 2:
            theirs, mine = product(tokens, both, offsets, width)
            other = to_core(theirs)
            if c == 0:
                fences[n_units - 3] = (theirs, mine)
        else:
            cut = len(both) - n_pieces
            partial = product([x[:-1] for x in tokens], both[:cut], offsets[:cut], width)
            last = functools.partial(product, pieces=both[cut:], offsets=offsets[cut:], width=width)
            other = to_core(last([tokens[0][-1:]], accs=partial[:1])[0])
            mine = last([tokens[1][-1:]], accs=partial[1:])[0]
        skip = 0
        if c == 0:
            skip = groups
            key, value = key_value(mine, other, bias, cosine, sine, columns[:groups], dtype)
        held = attention(
            mine, other, bias, cosine, sine, key, value, segments, held,
            columns[skip:], skip, base, groups * (HEADS // KV) * HD,
        )
        base += counts[c] - skip
        if c == 0:
            block_peak = peaks_here(qkv_weight, peaks, shared)
            fences[n_units - 1] = (held, block_peak)
    return held, block_peak


def solution(mesh):
    placed = (P("rep", None), P("rep", None), P(), P(("rep", "tp"), None), P())
    return jax.shard_map(
        shards,
        mesh=mesh,
        in_specs=placed,
        out_specs=(P("rep", "tp"), P(None, "tp")),
        check_vma=False,
    )
```

```python
import functools
import math

import jax
import jax.numpy as jnp
import numpy as np
from jax import lax
from jax.experimental import pallas as pl
from jax.experimental.pallas import tpu as pltpu
from jax.sharding import PartitionSpec as P

HEADS = 64
KV = 8
HD = 128
BLOCK = 128
UNIT = 2 * HD
PER_GROUP = (HEADS // KV + 2) * HD // UNIT

theta_base = 1000000.0
code_limit = 448.0
KERNEL_VMEM = 50 * 2**20


def after(value, *others):
    others = tuple(o for o in others if o is not None)
    return lax.optimization_barrier((value,) + others)[0] if others else value


def tile_scale(peak):
    return (peak + 1e-06) / code_limit


def tile_factor(scale):
    return (1.0 / scale) * (1.0 + 1.75e-07)


def restored_tile(tile, scale, factor):
    scaled = tile * factor
    lean = jnp.abs(scaled) * 0.750001
    wide = lean * (2.0**23 + 1.0)
    power = wide - (wide - lean)
    anchor = jnp.maximum(power * (1.5 * 2.0**20), 1.5 * 2.0**14)
    codes = (scaled + anchor) - anchor
    return codes * scale


def restore_kernel(views, table, *refs):
    count = len(refs) // (views + 1)
    sources, targets = refs[: count * views], refs[count * views :]
    tiles = []
    for n, source in enumerate(sources):
        target, shift = targets[n // views], n % views * UNIT
        for row in range(0, source.shape[0], BLOCK):
            for col in range(0, UNIT, BLOCK):
                here = (slice(row, row + BLOCK), slice(col, col + BLOCK))
                there = (here[0], slice(shift + col, shift + col + BLOCK))
                tiles.append((source, here, target, there))
    scales = []
    for source, here, _, _ in tiles:
        peak = jnp.max(jnp.abs(source[here]), axis=0, keepdims=True).astype(jnp.float32)
        scales.append(tile_scale(jnp.max(peak, axis=1, keepdims=True)))
    factors = [tile_factor(scale) for scale in scales]
    for (source, here, target, there), scale, factor in zip(tiles, scales, factors):
        tile = source[here].astype(jnp.float32)
        target[there] = restored_tile(tile, scale, factor).astype(target.dtype)


def restore(weight, table):
    rows = weight.shape[0]
    count, steps = table.shape
    views = 2 if count == 1 and steps % 2 == 0 else 1
    spec_in = [
        pl.BlockSpec(
            (rows, UNIT), functools.partial(lambda o, v, i, tab: (0, tab[o, i * views + v]), o, v)
        )
        for o in range(count)
        for v in range(views)
    ]
    return pl.pallas_call(
        functools.partial(restore_kernel, views),
        grid_spec=pltpu.PrefetchScalarGridSpec(
            num_scalar_prefetch=1,
            grid=(steps // views,),
            in_specs=spec_in,
            out_specs=[pl.BlockSpec((rows, views * UNIT), lambda i, tab: (0, i))] * count,
        ),
        out_shape=[jax.ShapeDtypeStruct((rows, steps * UNIT), weight.dtype)] * count,
        compiler_params=pltpu.CompilerParams(vmem_limit_bytes=KERNEL_VMEM),
        cost_estimate=pl.CostEstimate(
            flops=16 * rows * UNIT * steps * count,
            bytes_accessed=4 * rows * UNIT * steps * count,
            transcendentals=0,
        ),
    )(table, *([weight] * (count * views)))


def peaks_kernel(weight, fence, out):
    lanes = lax.broadcasted_iota(jnp.int32, out.shape, 1)
    sub = lax.broadcasted_iota(jnp.int32, out.shape, 0)

    def step(j, held):
        cols = pl.ds(pl.multiple_of(j * BLOCK, BLOCK), BLOCK)
        for row in range(weight.shape[0] // BLOCK):
            tile = jnp.abs(weight[row * BLOCK : (row + 1) * BLOCK, cols])
            peak = jnp.max(tile, axis=0, keepdims=True).astype(jnp.float32)
            peak = jnp.max(peak, axis=1, keepdims=True)
            held = jnp.where((lanes == j) & (sub == row), peak, held)
        return held

    out[...] = lax.fori_loop(
        0, weight.shape[1] // BLOCK, step, jnp.zeros(out.shape, jnp.float32), unroll=8
    )


def tile_peaks(weight, *others):
    rows, cols = weight.shape
    if rows % BLOCK == 0 and cols // BLOCK <= 128 and rows // BLOCK <= 8:
        held = pl.pallas_call(
            peaks_kernel,
            in_specs=[
                pl.BlockSpec((rows, cols), lambda: (0, 0)),
                pl.BlockSpec(memory_space=pltpu.SMEM),
            ],
            out_shape=jax.ShapeDtypeStruct((8, 128), jnp.float32),
            compiler_params=pltpu.CompilerParams(vmem_limit_bytes=KERNEL_VMEM),
            cost_estimate=pl.CostEstimate(
                flops=2 * rows * cols, bytes_accessed=2 * rows * cols, transcendentals=0
            ),
        )(weight, after(jnp.zeros((1,), jnp.int32), *others))
        return held[: rows // BLOCK, : cols // BLOCK].astype(weight.dtype)
    block = min(BLOCK, rows)
    view = jnp.abs(weight).reshape(rows // block, block, cols // BLOCK, BLOCK)
    return jnp.max(view, axis=(1, 3))


def shared_peaks(weight, shared):
    peaks = tile_peaks(weight)
    for bit in range(shared.bit_length() - 1):
        pairs = [(s, s ^ 2**bit) for s in range(lax.axis_size("tp"))]
        peaks = jnp.maximum(peaks, lax.ppermute(peaks, "tp", pairs))
    return peaks


def restore_plain(weight, peaks):
    rows, cols = weight.shape
    view = weight.astype(jnp.float32).reshape(
        peaks.shape[0], rows // peaks.shape[0], cols // BLOCK, BLOCK
    )
    scale = tile_scale(peaks.astype(jnp.float32)[:, None, :, None])
    held = restored_tile(view, scale, tile_factor(scale))
    return held.astype(weight.dtype).reshape(rows, cols)


def norm_kernel(block, table, hidden, gain, *outs):
    values = hidden[...].astype(jnp.float32)
    mean = jnp.sum(values * values, axis=-1, keepdims=True) * (1.0 / values.shape[1])
    inverse = lax.rsqrt(mean + 1e-06)
    for o, out in enumerate(outs):
        for b in range(out.shape[1] // block):
            cols = pl.ds(pl.multiple_of(table[o, b] * block, block), block)
            part = hidden[:, cols].astype(jnp.float32) * inverse * gain[:, cols]
            out[:, b * block : (b + 1) * block] = part.astype(out.dtype)


def norm(hidden, gain, table, block):
    tokens, depth = hidden.shape
    count, blocks = table.shape
    if block % 128 == 0:
        rows = min(64, tokens)
        return pl.pallas_call(
            functools.partial(norm_kernel, block),
            grid_spec=pltpu.PrefetchScalarGridSpec(
                num_scalar_prefetch=1,
                grid=(tokens // rows,),
                in_specs=[
                    pl.BlockSpec((rows, depth), lambda i, tab: (i, 0)),
                    pl.BlockSpec((1, depth), lambda i, tab: (0, 0)),
                ],
                out_specs=[pl.BlockSpec((rows, blocks * block), lambda i, tab: (i, 0))] * count,
            ),
            out_shape=[jax.ShapeDtypeStruct((tokens, blocks * block), hidden.dtype)] * count,
            compiler_params=pltpu.CompilerParams(vmem_limit_bytes=KERNEL_VMEM),
            cost_estimate=pl.CostEstimate(
                flops=6 * tokens * depth, bytes_accessed=4 * tokens * depth, transcendentals=0
            ),
        )(table, hidden, gain.astype(jnp.float32).reshape(1, depth))
    values = hidden.astype(jnp.float32)
    inverse = lax.rsqrt(jnp.mean(values * values, axis=-1, keepdims=True) + 1e-06)
    normed = (values * inverse * gain.astype(jnp.float32)).astype(hidden.dtype)
    view = normed.reshape(tokens, depth // block, block)
    return [jnp.take(view, table[o], axis=1).reshape(tokens, blocks * block) for o in range(count)]


def product_kernel(offsets, runs, n_x, n_acc, *refs):
    xs, refs = refs[: n_x * runs], refs[n_x * runs :]
    pieces, refs = refs[: len(offsets)], refs[len(offsets) :]
    accs, refs = refs[:n_acc], refs[n_acc:]
    outs, (x_held, w_held, x_sems, w_sems) = refs[:n_x], refs[n_x:]
    height, width = pieces[0].shape[0], outs[0].shape[1]
    group = len(pieces) // runs
    copies = []
    for r in range(runs):
        own = [
            pltpu.make_async_copy(xs[n * runs + r], x_held.at[n, r], x_sems.at[n, r])
            for n in range(n_x)
        ]
        for p in range(r * group, (r + 1) * group):
            own.append(
                pltpu.make_async_copy(
                    pieces[p].at[:, pl.ds(offsets[p], width)],
                    w_held.at[r, pl.ds((p - r * group) * height, height), :],
                    w_sems.at[p],
                )
            )
        copies.append(own)
        for copy in own:
            copy.start()
    for r in range(runs):
        for copy in copies[r]:
            copy.wait()
        for n, out in enumerate(outs):
            part = jnp.dot(x_held[n, r], w_held[r], preferred_element_type=jnp.float32)
            if r > 0:
                part = out[...] + part
            elif n_acc:
                part = accs[n][...] + part
            out[...] = part


def product(xs, pieces, offsets, width, accs=()):
    runs = len(xs[0])
    tokens, depth = xs[0][0].shape
    if pieces[0].shape[0] % 128:
        held = jnp.concatenate([p[:, o : o + width] for p, o in zip(pieces, offsets)], axis=0)
        outs = [
            jnp.dot(jnp.concatenate(x, axis=1), held, preferred_element_type=jnp.float32) for x in xs
        ]
        return [a + o for a, o in zip(accs, outs)] if accs else outs
    count = len(xs)
    return pl.pallas_call(
        functools.partial(product_kernel, tuple(offsets), runs, count, len(accs)),
        in_specs=[pl.BlockSpec(memory_space=pl.ANY)] * (count * runs + len(pieces))
        + [pl.BlockSpec(memory_space=pltpu.VMEM)] * len(accs),
        out_specs=[pl.BlockSpec(memory_space=pltpu.VMEM)] * count,
        out_shape=[jax.ShapeDtypeStruct((tokens, width), jnp.float32)] * count,
        scratch_shapes=[
            pltpu.VMEM((count, runs, tokens, depth), pieces[0].dtype),
            pltpu.VMEM((runs, depth, width), pieces[0].dtype),
            pltpu.SemaphoreType.DMA((count, runs)),
            pltpu.SemaphoreType.DMA((len(pieces),)),
        ],
        compiler_params=pltpu.CompilerParams(vmem_limit_bytes=KERNEL_VMEM),
        cost_estimate=pl.CostEstimate(
            flops=2 * count * tokens * runs * depth * width,
            bytes_accessed=2 * runs * depth * (count * tokens + width) + 4 * count * tokens * width,
            transcendentals=0,
        ),
    )(*[part for x in xs for part in x], *pieces, *accs)


def token_positions(segments):
    index = jnp.arange(segments.shape[0], dtype=jnp.int32)
    same = (segments[:, None] == segments[None, :]) & (index[None, :] < index[:, None])
    return jnp.sum(same.astype(jnp.int32), axis=1)


def rotary_tables(position):
    half = HD // 2
    index = jnp.arange(half, dtype=jnp.float32)
    frequency = jnp.exp(index * (-2.0 / HD) * math.log(theta_base))
    angles = position.astype(jnp.float32)[:, None] * frequency[None, :]
    cosine, sine = jnp.cos(angles), jnp.sin(angles)
    return (
        jnp.concatenate([cosine, cosine], axis=1),
        jnp.concatenate([-sine, sine], axis=1),
    )


def rotate(head, cosine, sine):
    return head * cosine + pltpu.roll(head, HD // 2, 1) * sine


def key_value_kernel(table, own, other, bias, cosine, sine, key, value):
    both = own[...] + other[...] + bias[...]
    key[...] = rotate(both[:, :HD], cosine[...], sine[...]).astype(key.dtype)
    value[...] = both[:, HD:].astype(value.dtype)


def key_value(own, other, bias, cosine, sine, table, dtype):
    tokens = own.shape[0]
    groups = table.shape[0]
    half = pl.BlockSpec((tokens, UNIT), lambda i, tab: (0, i))
    whole = pl.BlockSpec((tokens, HD), lambda i, tab: (0, 0))
    head = pl.BlockSpec((tokens, HD), lambda i, tab: (0, i))
    return pl.pallas_call(
        key_value_kernel,
        grid_spec=pltpu.PrefetchScalarGridSpec(
            num_scalar_prefetch=1,
            grid=(groups,),
            in_specs=[half, half, pl.BlockSpec((1, UNIT), lambda i, tab: (0, tab[i])), whole, whole],
            out_specs=[head, head],
        ),
        out_shape=[jax.ShapeDtypeStruct((tokens, groups * HD), dtype)] * 2,
        compiler_params=pltpu.CompilerParams(vmem_limit_bytes=KERNEL_VMEM),
        cost_estimate=pl.CostEstimate(
            flops=6 * tokens * groups * UNIT, bytes_accessed=10 * tokens * groups * UNIT, transcendentals=0
        ),
    )(table, own, other, bias, cosine, sine)


def attention_kernel(views, table, own, other, *refs):
    biases, (cosine, sine, key, value, seg_rows, seg_cols, _, out) = refs[:views], refs[views:]
    tokens = own.shape[0]
    rows = min(128, tokens)
    scale = math.log2(math.e) / math.sqrt(HD)
    queries = []
    for h in range(own.shape[1] // HD):
        cols = slice(h * HD, (h + 1) * HD)
        bias = biases[h * HD // UNIT][:, h * HD % UNIT : h * HD % UNIT + HD]
        query = own[:, cols] + other[:, cols] + bias
        queries.append(rotate(query, cosine[...], sine[...]).astype(key.dtype))
    count = len(queries)
    for first in range(0, tokens, rows):
        low, high = max(0, first - 256), first + rows
        row = first + lax.broadcasted_iota(jnp.int32, (rows, high - low), 0)
        col = low + lax.broadcasted_iota(jnp.int32, (rows, high - low), 1)
        allowed = (seg_rows[first:high, :] == seg_cols[:, low:high]) & (col <= row)
        scores = lax.dot_general(
            jnp.concatenate([query[first:high, :] for query in queries], axis=0),
            key[low:high, :],
            (((1,), (1,)), ((), ())),
            preferred_element_type=jnp.float32,
        )
        scores = jnp.where(allowed[None], scores.reshape(count, rows, high - low), -1e30)
        weights = jnp.exp2((scores - jnp.max(scores, axis=-1, keepdims=True)) * scale)
        total = jnp.sum(weights, axis=-1, keepdims=True)
        chances = (weights * (1.0 / total)).astype(value.dtype)
        mixed = jnp.dot(
            chances.reshape(count * rows, high - low),
            value[low:high, :],
            preferred_element_type=jnp.float32,
        ).astype(out.dtype)
        for h in range(count):
            out[first:high, h * HD : (h + 1) * HD] = mixed[h * rows : (h + 1) * rows]


def attention(own, other, bias, cosine, sine, key, value, segments, held, table, skip, base, width):
    tokens = own.shape[0]
    count = table.shape[0]
    per_group = HEADS // KV * HD // UNIT
    views = 2 if count % 2 == skip % 2 == base % 2 == 0 else 1
    half = pl.BlockSpec((tokens, views * UNIT), lambda i, tab: (0, skip // views + i))
    whole = pl.BlockSpec((tokens, HD), lambda i, tab: (0, 0))
    head = pl.BlockSpec((tokens, HD), lambda i, tab: (0, (base + i * views) // per_group))
    in_specs = [
        half,
        half,
        *[
            pl.BlockSpec((1, UNIT), functools.partial(lambda v, i, tab: (0, tab[i * views + v]), v))
            for v in range(views)
        ],
        whole,
        whole,
        head,
        head,
        pl.BlockSpec((tokens, 1), lambda i, tab: (0, 0)),
        pl.BlockSpec((1, tokens), lambda i, tab: (0, 0)),
    ]
    args = [table, own, other, *[bias] * views, cosine, sine, key, value]
    args += [segments[:, None], segments[None, :]]
    aliases = {}
    body = functools.partial(attention_kernel, views)
    if held is None:
        body = lambda *refs: attention_kernel(views, *refs[:-1], None, refs[-1])
    else:
        in_specs.append(pl.BlockSpec(memory_space=pl.ANY))
        args.append(held)
        aliases = {len(args) - 1: 0}
    return pl.pallas_call(
        body,
        grid_spec=pltpu.PrefetchScalarGridSpec(
            num_scalar_prefetch=1,
            grid=(count // views,),
            in_specs=in_specs,
            out_specs=pl.BlockSpec((tokens, views * UNIT), lambda i, tab: (0, base // views + i)),
        ),
        out_shape=jax.ShapeDtypeStruct((tokens, width), key.dtype),
        input_output_aliases=aliases,
        compiler_params=pltpu.CompilerParams(vmem_limit_bytes=KERNEL_VMEM),
        cost_estimate=pl.CostEstimate(
            flops=4 * tokens * tokens * UNIT * count,
            bytes_accessed=8 * tokens * UNIT * count,
            transcendentals=tokens * tokens * 2 * count,
        ),
    )(*args)


def peaks_here(weight, peaks, shared, *others):
    n_rep, n_tp = lax.axis_size("rep"), lax.axis_size("tp")
    rep, tp = lax.axis_index("rep"), lax.axis_index("tp")
    if peaks is None:
        peaks = tile_peaks(weight, *others)
    blocks, tiles = peaks.shape
    bits = []
    for name, size, index in (("tp", n_tp, tp), ("rep", n_rep, rep)):
        for bit in range(size.bit_length() - 1):
            pairs = [(d, d ^ 2**bit) for d in range(size)]
            peaks = jnp.concatenate([peaks, lax.ppermute(peaks, name, pairs)], axis=0)
            bits.append((index >> bit) % 2 == 1)
    here = lax.dynamic_slice_in_dim(peaks, tp * (tiles // n_tp), tiles // n_tp, 1)
    here = here.reshape((2,) * len(bits) + (blocks, tiles // n_tp))
    for axis, bit in enumerate(reversed(bits)):
        here = jnp.where(bit, jnp.flip(here, axis), here)
    return here.reshape(-1, tiles // n_tp)[::shared]


def shards(hidden, segment_ids, norm_gain, qkv_weight, qkv_bias):
    n_rep, n_tp = lax.axis_size("rep"), lax.axis_size("tp")
    rep, tp = lax.axis_index("rep"), lax.axis_index("tp")
    rows, full_width = qkv_weight.shape
    shared = max(1, BLOCK // rows)
    groups = KV // n_tp
    local_units = groups * PER_GROUP
    dtype = qkv_weight.dtype

    bits = [2**b for b in range(1, n_rep.bit_length() - 1)]
    n_pieces = 2 ** len(bits)
    core = rep % 2

    def bit_of(step, of_core):
        return bits[(of_core + step) % len(bits)]

    def gather_step(value, step):
        return lax.ppermute(value, "rep", [(r, r ^ bit_of(step, r % 2)) for r in range(n_rep)])

    def to_core(value):
        return lax.ppermute(value, "rep", [(r, r ^ 1) for r in range(n_rep)])

    def to_server(value, shift):
        return lax.ppermute(value, "tp", [(t, (t + shift) % n_tp) for t in range(n_tp)])

    value_units = [g * PER_GROUP + PER_GROUP - 1 for g in range(groups)]
    query_units = [u for u in range(local_units) if u not in value_units]
    order = np.array(value_units + query_units, np.int32)
    counts = [2 * groups, 2 * groups, groups]
    starts = [0, counts[0], counts[0] + counts[1]]

    if shared == 1 and rows % BLOCK == 0:
        peaks = None

        def restored_units(shifts, first, count, *others):
            units = jnp.asarray(order[first : first + count])
            servers = (tp + jnp.asarray(shifts, jnp.int32)) % n_tp
            table = servers[:, None] * local_units + units[None, :]
            return restore(qkv_weight, after(table, *others))

    else:
        peaks = shared_peaks(qkv_weight, shared)
        plain = restore_plain(qkv_weight, peaks).reshape(rows, n_tp, local_units, UNIT)

        def restored_units(shifts, first, count, *others):
            out = []
            for shift in shifts:
                part = lax.dynamic_index_in_dim(plain, (tp + shift) % n_tp, 1, keepdims=False)
                out.append(part[:, order[first : first + count]].reshape(rows, count * UNIT))
            return out

    far = list(range(1, n_tp))
    n_far = len(far)
    own_a = restored_units([0], 0, counts[0])[0]
    far_units = restored_units(far, 0, counts[0]) if far else []
    step_masks = range(n_pieces)
    relative = np.zeros((2, n_pieces), np.int32)
    for k in range(2):
        for m in step_masks:
            for s in range(len(bits)):
                if m >> s & 1:
                    relative[k, m] ^= bit_of(s, k)
    relative = jnp.asarray(relative)
    shifts = jnp.arange(n_tp, dtype=jnp.int32)

    def depth_blocks(of_rep):
        source = of_rep ^ relative[of_rep % 2]
        server = (tp - shifts) % n_tp
        return (source[None, :] * n_tp + server[:, None]).reshape(-1)

    table = jnp.concatenate(
        [depth_blocks(r).reshape(n_tp, n_pieces) for r in (rep, rep ^ 1)], axis=0
    )
    pieces = []
    served = {}
    fences = {}
    n_units = 2 + 3 * n_far

    def arrived(u):
        return () if u < 0 else tuple(pieces[u][1:-1]) + (tuple(pieces[u - 1][-1:]) if u > 0 else ())

    def near(u):
        return pieces[u][min(1, n_pieces - 1)]

    def serve(u, held):
        fence = (near(u - 4),) if u >= 4 else ()
        served[u] = to_server(after(held, *fence), far[(u - 2) % n_far])

    def gather(held):
        u = len(pieces)
        got = [after(held, *arrived(u - 2), *fences.get(u, ()))]
        for step in range(len(bits)):
            got += [gather_step(g, step) for g in got]
        pieces.append(got)

    gather(own_a)
    for u in range(2, 2 + min(n_far, 3)):
        serve(u, far_units[u - 2])
    own_b = restored_units([0], counts[0], counts[1] + counts[2])[0]
    gather(own_b)
    far_units += restored_units(far, starts[1], counts[1])
    far_units += restored_units(far, starts[2], counts[2])
    parts = norm(hidden, norm_gain, table, rows)
    tokens = [[to_core(p) for p in parts[n_tp:]], parts[:n_tp]]
    segments = segment_ids[0]
    cosine, sine = rotary_tables(token_positions(segments))
    bias = qkv_bias.astype(jnp.float32).reshape(1, full_width)
    held = key = value = None
    base = 0
    for c in range(3):
        width = counts[c] * UNIT
        offset = (starts[c] - starts[min(c, 1)]) * UNIT
        columns = tp * local_units + jnp.asarray(order[starts[c] : starts[c] + counts[c]])
        for n in range(n_far):
            u = len(pieces)
            if u not in served:
                serve(u, far_units[u - 2])
            gather(served[u])
        chunk = [p for got in pieces[2 + c * n_far :] for p in got]
        both = pieces[min(c, 1)] + chunk
        offsets = [offset] * n_pieces + [0] * len(chunk)
        if c < 2:
            theirs, mine = product(tokens, both, offsets, width)
            other = to_core(theirs)
            if c == 0:
                fences[n_units - 2] = (theirs, mine)
        else:
            cut = len(both) - n_pieces
            partial = product([x[:-1] for x in tokens], both[:cut], offsets[:cut], width)
            last = functools.partial(product, pieces=both[cut:], offsets=offsets[cut:], width=width)
            other = to_core(last([tokens[0][-1:]], accs=partial[:1])[0])
            mine = last([tokens[1][-1:]], accs=partial[1:])[0]
        skip = 0
        if c == 0:
            skip = groups
            key, value = key_value(mine, other, bias, cosine, sine, columns[:groups], dtype)
        held = attention(
            mine, other, bias, cosine, sine, key, value, segments, held,
            columns[skip:], skip, base, groups * (HEADS // KV) * HD,
        )
        base += counts[c] - skip
        if c == 0:
            block_peak = peaks_here(qkv_weight, peaks, shared)
            fences[n_units - 1] = (held,)
            fences[n_units - 2] = fences.get(n_units - 2, ()) + (block_peak,)
    return held, block_peak


def solution(mesh):
    placed = (P("rep", None), P("rep", None), P(), P(("rep", "tp"), None), P())
    return jax.shard_map(
        shards,
        mesh=mesh,
        in_specs=placed,
        out_specs=(P("rep", "tp"), P(None, "tp")),
        check_vma=False,
    )
```

```python
import functools
import math

import jax
import jax.numpy as jnp
import numpy as np
from jax import lax
from jax.experimental import pallas as pl
from jax.experimental.pallas import tpu as pltpu
from jax.sharding import PartitionSpec as P

HEADS = 64
KV = 8
HD = 128
BLOCK = 128
UNIT = 2 * HD
PER_GROUP = (HEADS // KV + 2) * HD // UNIT

theta_base = 1000000.0
code_limit = 448.0
KERNEL_VMEM = 50 * 2**20


def after(value, *others):
    others = tuple(o for o in others if o is not None)
    return lax.optimization_barrier((value,) + others)[0] if others else value


def tile_scale(peak):
    return (peak + 1e-06) / code_limit


def tile_factor(scale):
    return (1.0 / scale) * (1.0 + 1.75e-07)


def restored_tile(tile, scale, factor):
    scaled = tile * factor
    lean = jnp.abs(scaled) * 0.750001
    wide = lean * (2.0**23 + 1.0)
    power = wide - (wide - lean)
    anchor = jnp.maximum(power * (1.5 * 2.0**20), 1.5 * 2.0**14)
    codes = (scaled + anchor) - anchor
    return codes * scale


def restore_kernel(views, table, *refs):
    count = len(refs) // (views + 1)
    sources, targets = refs[: count * views], refs[count * views :]
    tiles = []
    for n, source in enumerate(sources):
        target, shift = targets[n // views], n % views * UNIT
        for row in range(0, source.shape[0], BLOCK):
            for col in range(0, UNIT, BLOCK):
                here = (slice(row, row + BLOCK), slice(col, col + BLOCK))
                there = (here[0], slice(shift + col, shift + col + BLOCK))
                tiles.append((source, here, target, there))
    scales = []
    for source, here, _, _ in tiles:
        peak = jnp.max(jnp.abs(source[here]), axis=0, keepdims=True).astype(jnp.float32)
        scales.append(tile_scale(jnp.max(peak, axis=1, keepdims=True)))
    factors = [tile_factor(scale) for scale in scales]
    for (source, here, target, there), scale, factor in zip(tiles, scales, factors):
        tile = source[here].astype(jnp.float32)
        target[there] = restored_tile(tile, scale, factor).astype(target.dtype)


def restore(weight, table):
    rows = weight.shape[0]
    count, steps = table.shape
    views = 2 if count == 1 and steps % 2 == 0 else 1
    spec_in = [
        pl.BlockSpec(
            (rows, UNIT), functools.partial(lambda o, v, i, tab: (0, tab[o, i * views + v]), o, v)
        )
        for o in range(count)
        for v in range(views)
    ]
    return pl.pallas_call(
        functools.partial(restore_kernel, views),
        grid_spec=pltpu.PrefetchScalarGridSpec(
            num_scalar_prefetch=1,
            grid=(steps // views,),
            in_specs=spec_in,
            out_specs=[pl.BlockSpec((rows, views * UNIT), lambda i, tab: (0, i))] * count,
        ),
        out_shape=[jax.ShapeDtypeStruct((rows, steps * UNIT), weight.dtype)] * count,
        compiler_params=pltpu.CompilerParams(vmem_limit_bytes=KERNEL_VMEM),
        cost_estimate=pl.CostEstimate(
            flops=16 * rows * UNIT * steps * count,
            bytes_accessed=4 * rows * UNIT * steps * count,
            transcendentals=0,
        ),
    )(table, *([weight] * (count * views)))


def peaks_kernel(weight, fence, out):
    lanes = lax.broadcasted_iota(jnp.int32, out.shape, 1)
    sub = lax.broadcasted_iota(jnp.int32, out.shape, 0)

    def step(j, held):
        cols = pl.ds(pl.multiple_of(j * BLOCK, BLOCK), BLOCK)
        for row in range(weight.shape[0] // BLOCK):
            tile = jnp.abs(weight[row * BLOCK : (row + 1) * BLOCK, cols])
            peak = jnp.max(tile, axis=0, keepdims=True).astype(jnp.float32)
            peak = jnp.max(peak, axis=1, keepdims=True)
            held = jnp.where((lanes == j) & (sub == row), peak, held)
        return held

    out[...] = lax.fori_loop(
        0, weight.shape[1] // BLOCK, step, jnp.zeros(out.shape, jnp.float32), unroll=8
    )


def tile_peaks(weight, *others):
    rows, cols = weight.shape
    if rows % BLOCK == 0 and cols // BLOCK <= 128 and rows // BLOCK <= 8:
        held = pl.pallas_call(
            peaks_kernel,
            in_specs=[
                pl.BlockSpec((rows, cols), lambda: (0, 0)),
                pl.BlockSpec(memory_space=pltpu.SMEM),
            ],
            out_shape=jax.ShapeDtypeStruct((8, 128), jnp.float32),
            compiler_params=pltpu.CompilerParams(vmem_limit_bytes=KERNEL_VMEM),
            cost_estimate=pl.CostEstimate(
                flops=2 * rows * cols, bytes_accessed=2 * rows * cols, transcendentals=0
            ),
        )(weight, after(jnp.zeros((1,), jnp.int32), *others))
        return held[: rows // BLOCK, : cols // BLOCK].astype(weight.dtype)
    block = min(BLOCK, rows)
    view = jnp.abs(weight).reshape(rows // block, block, cols // BLOCK, BLOCK)
    return jnp.max(view, axis=(1, 3))


def shared_peaks(weight, shared):
    peaks = tile_peaks(weight)
    for bit in range(shared.bit_length() - 1):
        pairs = [(s, s ^ 2**bit) for s in range(lax.axis_size("tp"))]
        peaks = jnp.maximum(peaks, lax.ppermute(peaks, "tp", pairs))
    return peaks


def restore_plain(weight, peaks):
    rows, cols = weight.shape
    view = weight.astype(jnp.float32).reshape(
        peaks.shape[0], rows // peaks.shape[0], cols // BLOCK, BLOCK
    )
    scale = tile_scale(peaks.astype(jnp.float32)[:, None, :, None])
    held = restored_tile(view, scale, tile_factor(scale))
    return held.astype(weight.dtype).reshape(rows, cols)


def norm_kernel(block, table, hidden, gain, *outs):
    values = hidden[...].astype(jnp.float32)
    mean = jnp.sum(values * values, axis=-1, keepdims=True) * (1.0 / values.shape[1])
    inverse = lax.rsqrt(mean + 1e-06)
    for o, out in enumerate(outs):
        for b in range(out.shape[1] // block):
            cols = pl.ds(pl.multiple_of(table[o, b] * block, block), block)
            part = hidden[:, cols].astype(jnp.float32) * inverse * gain[:, cols]
            out[:, b * block : (b + 1) * block] = part.astype(out.dtype)


def norm(hidden, gain, table, block):
    tokens, depth = hidden.shape
    count, blocks = table.shape
    if block % 128 == 0:
        rows = min(64, tokens)
        return pl.pallas_call(
            functools.partial(norm_kernel, block),
            grid_spec=pltpu.PrefetchScalarGridSpec(
                num_scalar_prefetch=1,
                grid=(tokens // rows,),
                in_specs=[
                    pl.BlockSpec((rows, depth), lambda i, tab: (i, 0)),
                    pl.BlockSpec((1, depth), lambda i, tab: (0, 0)),
                ],
                out_specs=[pl.BlockSpec((rows, blocks * block), lambda i, tab: (i, 0))] * count,
            ),
            out_shape=[jax.ShapeDtypeStruct((tokens, blocks * block), hidden.dtype)] * count,
            compiler_params=pltpu.CompilerParams(vmem_limit_bytes=KERNEL_VMEM),
            cost_estimate=pl.CostEstimate(
                flops=6 * tokens * depth, bytes_accessed=4 * tokens * depth, transcendentals=0
            ),
        )(table, hidden, gain.astype(jnp.float32).reshape(1, depth))
    values = hidden.astype(jnp.float32)
    inverse = lax.rsqrt(jnp.mean(values * values, axis=-1, keepdims=True) + 1e-06)
    normed = (values * inverse * gain.astype(jnp.float32)).astype(hidden.dtype)
    view = normed.reshape(tokens, depth // block, block)
    return [jnp.take(view, table[o], axis=1).reshape(tokens, blocks * block) for o in range(count)]


def product_kernel(offsets, runs, n_x, n_acc, *refs):
    xs, refs = refs[: n_x * runs], refs[n_x * runs :]
    pieces, refs = refs[: len(offsets)], refs[len(offsets) :]
    accs, refs = refs[:n_acc], refs[n_acc:]
    outs, (x_held, w_held, x_sems, w_sems) = refs[:n_x], refs[n_x:]
    height, width = pieces[0].shape[0], outs[0].shape[1]
    group = len(pieces) // runs
    copies = []
    for r in range(runs):
        own = [
            pltpu.make_async_copy(xs[n * runs + r], x_held.at[n, r], x_sems.at[n, r])
            for n in range(n_x)
        ]
        for p in range(r * group, (r + 1) * group):
            own.append(
                pltpu.make_async_copy(
                    pieces[p].at[:, pl.ds(offsets[p], width)],
                    w_held.at[r, pl.ds((p - r * group) * height, height), :],
                    w_sems.at[p],
                )
            )
        copies.append(own)
    for copy in [c for own in copies[:2] for c in own]:
        copy.start()
    for r in range(runs):
        for copy in copies[r]:
            copy.wait()
        for copy in copies[r + 2] if r + 2 < runs else []:
            copy.start()
        for n, out in enumerate(outs):
            part = jnp.dot(x_held[n, r], w_held[r], preferred_element_type=jnp.float32)
            if r > 0:
                part = out[...] + part
            elif n_acc:
                part = accs[n][...] + part
            out[...] = part


def product(xs, pieces, offsets, width, accs=()):
    runs = len(xs[0])
    tokens, depth = xs[0][0].shape
    if pieces[0].shape[0] % 128:
        held = jnp.concatenate([p[:, o : o + width] for p, o in zip(pieces, offsets)], axis=0)
        outs = [
            jnp.dot(jnp.concatenate(x, axis=1), held, preferred_element_type=jnp.float32) for x in xs
        ]
        return [a + o for a, o in zip(accs, outs)] if accs else outs
    count = len(xs)
    return pl.pallas_call(
        functools.partial(product_kernel, tuple(offsets), runs, count, len(accs)),
        in_specs=[pl.BlockSpec(memory_space=pl.ANY)] * (count * runs + len(pieces))
        + [pl.BlockSpec(memory_space=pltpu.VMEM)] * len(accs),
        out_specs=[pl.BlockSpec(memory_space=pltpu.VMEM)] * count,
        out_shape=[jax.ShapeDtypeStruct((tokens, width), jnp.float32)] * count,
        scratch_shapes=[
            pltpu.VMEM((count, runs, tokens, depth), pieces[0].dtype),
            pltpu.VMEM((runs, depth, width), pieces[0].dtype),
            pltpu.SemaphoreType.DMA((count, runs)),
            pltpu.SemaphoreType.DMA((len(pieces),)),
        ],
        compiler_params=pltpu.CompilerParams(vmem_limit_bytes=KERNEL_VMEM),
        cost_estimate=pl.CostEstimate(
            flops=2 * count * tokens * runs * depth * width,
            bytes_accessed=2 * runs * depth * (count * tokens + width) + 4 * count * tokens * width,
            transcendentals=0,
        ),
    )(*[part for x in xs for part in x], *pieces, *accs)


def token_positions(segments):
    index = jnp.arange(segments.shape[0], dtype=jnp.int32)
    same = (segments[:, None] == segments[None, :]) & (index[None, :] < index[:, None])
    return jnp.sum(same.astype(jnp.int32), axis=1)


def rotary_tables(position):
    half = HD // 2
    index = jnp.arange(half, dtype=jnp.float32)
    frequency = jnp.exp(index * (-2.0 / HD) * math.log(theta_base))
    angles = position.astype(jnp.float32)[:, None] * frequency[None, :]
    cosine, sine = jnp.cos(angles), jnp.sin(angles)
    return (
        jnp.concatenate([cosine, cosine], axis=1),
        jnp.concatenate([-sine, sine], axis=1),
    )


def rotate(head, cosine, sine):
    return head * cosine + pltpu.roll(head, HD // 2, 1) * sine


def key_value_kernel(table, own, other, bias, cosine, sine, key, value):
    both = own[...] + other[...] + bias[...]
    key[...] = rotate(both[:, :HD], cosine[...], sine[...]).astype(key.dtype)
    value[...] = both[:, HD:].astype(value.dtype)


def key_value(own, other, bias, cosine, sine, table, dtype):
    tokens = own.shape[0]
    groups = table.shape[0]
    half = pl.BlockSpec((tokens, UNIT), lambda i, tab: (0, i))
    whole = pl.BlockSpec((tokens, HD), lambda i, tab: (0, 0))
    head = pl.BlockSpec((tokens, HD), lambda i, tab: (0, i))
    return pl.pallas_call(
        key_value_kernel,
        grid_spec=pltpu.PrefetchScalarGridSpec(
            num_scalar_prefetch=1,
            grid=(groups,),
            in_specs=[half, half, pl.BlockSpec((1, UNIT), lambda i, tab: (0, tab[i])), whole, whole],
            out_specs=[head, head],
        ),
        out_shape=[jax.ShapeDtypeStruct((tokens, groups * HD), dtype)] * 2,
        compiler_params=pltpu.CompilerParams(vmem_limit_bytes=KERNEL_VMEM),
        cost_estimate=pl.CostEstimate(
            flops=6 * tokens * groups * UNIT, bytes_accessed=10 * tokens * groups * UNIT, transcendentals=0
        ),
    )(table, own, other, bias, cosine, sine)


def attention_kernel(views, table, own, other, *refs):
    biases, (cosine, sine, key, value, seg_rows, seg_cols, _, out) = refs[:views], refs[views:]
    tokens = own.shape[0]
    rows = min(128, tokens)
    scale = math.log2(math.e) / math.sqrt(HD)
    queries = []
    for h in range(own.shape[1] // HD):
        cols = slice(h * HD, (h + 1) * HD)
        bias = biases[h * HD // UNIT][:, h * HD % UNIT : h * HD % UNIT + HD]
        query = own[:, cols] + other[:, cols] + bias
        queries.append(rotate(query, cosine[...], sine[...]).astype(key.dtype))
    count = len(queries)
    for first in range(0, tokens, rows):
        low, high = max(0, first - 256), first + rows
        row = first + lax.broadcasted_iota(jnp.int32, (rows, high - low), 0)
        col = low + lax.broadcasted_iota(jnp.int32, (rows, high - low), 1)
        allowed = (seg_rows[first:high, :] == seg_cols[:, low:high]) & (col <= row)
        scores = lax.dot_general(
            jnp.concatenate([query[first:high, :] for query in queries], axis=0),
            key[low:high, :],
            (((1,), (1,)), ((), ())),
            preferred_element_type=jnp.float32,
        )
        scores = jnp.where(allowed[None], scores.reshape(count, rows, high - low), -1e30)
        weights = jnp.exp2((scores - jnp.max(scores, axis=-1, keepdims=True)) * scale)
        total = jnp.sum(weights, axis=-1, keepdims=True)
        chances = (weights * (1.0 / total)).astype(value.dtype)
        mixed = jnp.dot(
            chances.reshape(count * rows, high - low),
            value[low:high, :],
            preferred_element_type=jnp.float32,
        ).astype(out.dtype)
        for h in range(count):
            out[first:high, h * HD : (h + 1) * HD] = mixed[h * rows : (h + 1) * rows]


def attention(own, other, bias, cosine, sine, key, value, segments, held, table, skip, base, width):
    tokens = own.shape[0]
    count = table.shape[0]
    per_group = HEADS // KV * HD // UNIT
    views = 2 if count % 2 == skip % 2 == base % 2 == 0 else 1
    half = pl.BlockSpec((tokens, views * UNIT), lambda i, tab: (0, skip // views + i))
    whole = pl.BlockSpec((tokens, HD), lambda i, tab: (0, 0))
    head = pl.BlockSpec((tokens, HD), lambda i, tab: (0, (base + i * views) // per_group))
    in_specs = [
        half,
        half,
        *[
            pl.BlockSpec((1, UNIT), functools.partial(lambda v, i, tab: (0, tab[i * views + v]), v))
            for v in range(views)
        ],
        whole,
        whole,
        head,
        head,
        pl.BlockSpec((tokens, 1), lambda i, tab: (0, 0)),
        pl.BlockSpec((1, tokens), lambda i, tab: (0, 0)),
    ]
    args = [table, own, other, *[bias] * views, cosine, sine, key, value]
    args += [segments[:, None], segments[None, :]]
    aliases = {}
    body = functools.partial(attention_kernel, views)
    if held is None:
        body = lambda *refs: attention_kernel(views, *refs[:-1], None, refs[-1])
    else:
        in_specs.append(pl.BlockSpec(memory_space=pl.ANY))
        args.append(held)
        aliases = {len(args) - 1: 0}
    return pl.pallas_call(
        body,
        grid_spec=pltpu.PrefetchScalarGridSpec(
            num_scalar_prefetch=1,
            grid=(count // views,),
            in_specs=in_specs,
            out_specs=pl.BlockSpec((tokens, views * UNIT), lambda i, tab: (0, base // views + i)),
        ),
        out_shape=jax.ShapeDtypeStruct((tokens, width), key.dtype),
        input_output_aliases=aliases,
        compiler_params=pltpu.CompilerParams(vmem_limit_bytes=KERNEL_VMEM),
        cost_estimate=pl.CostEstimate(
            flops=4 * tokens * tokens * UNIT * count,
            bytes_accessed=8 * tokens * UNIT * count,
            transcendentals=tokens * tokens * 2 * count,
        ),
    )(*args)


def peaks_here(weight, peaks, shared, *others):
    n_rep, n_tp = lax.axis_size("rep"), lax.axis_size("tp")
    rep, tp = lax.axis_index("rep"), lax.axis_index("tp")
    if peaks is None:
        peaks = tile_peaks(weight, *others)
    blocks, tiles = peaks.shape
    bits = []
    for name, size, index in (("tp", n_tp, tp), ("rep", n_rep, rep)):
        for bit in range(size.bit_length() - 1):
            pairs = [(d, d ^ 2**bit) for d in range(size)]
            peaks = jnp.concatenate([peaks, lax.ppermute(peaks, name, pairs)], axis=0)
            bits.append((index >> bit) % 2 == 1)
    here = lax.dynamic_slice_in_dim(peaks, tp * (tiles // n_tp), tiles // n_tp, 1)
    here = here.reshape((2,) * len(bits) + (blocks, tiles // n_tp))
    for axis, bit in enumerate(reversed(bits)):
        here = jnp.where(bit, jnp.flip(here, axis), here)
    return here.reshape(-1, tiles // n_tp)[::shared]


def shards(hidden, segment_ids, norm_gain, qkv_weight, qkv_bias):
    n_rep, n_tp = lax.axis_size("rep"), lax.axis_size("tp")
    rep, tp = lax.axis_index("rep"), lax.axis_index("tp")
    rows, full_width = qkv_weight.shape
    shared = max(1, BLOCK // rows)
    groups = KV // n_tp
    local_units = groups * PER_GROUP
    dtype = qkv_weight.dtype

    bits = [2**b for b in range(1, n_rep.bit_length() - 1)]
    n_pieces = 2 ** len(bits)
    core = rep % 2

    def bit_of(step, of_core):
        return bits[(of_core + step) % len(bits)]

    def gather_step(value, step):
        return lax.ppermute(value, "rep", [(r, r ^ bit_of(step, r % 2)) for r in range(n_rep)])

    def to_core(value):
        return lax.ppermute(value, "rep", [(r, r ^ 1) for r in range(n_rep)])

    def to_server(value, shift):
        return lax.ppermute(value, "tp", [(t, (t + shift) % n_tp) for t in range(n_tp)])

    value_units = [g * PER_GROUP + PER_GROUP - 1 for g in range(groups)]
    query_units = [u for u in range(local_units) if u not in value_units]
    order = np.array(value_units + query_units, np.int32)
    counts = [2 * groups, 2 * groups, groups]
    starts = [0, counts[0], counts[0] + counts[1]]

    if shared == 1 and rows % BLOCK == 0:
        peaks = None

        def restored_units(shifts, first, count, *others):
            units = jnp.asarray(order[first : first + count])
            servers = (tp + jnp.asarray(shifts, jnp.int32)) % n_tp
            table = servers[:, None] * local_units + units[None, :]
            return restore(qkv_weight, after(table, *others))

    else:
        peaks = shared_peaks(qkv_weight, shared)
        plain = restore_plain(qkv_weight, peaks).reshape(rows, n_tp, local_units, UNIT)

        def restored_units(shifts, first, count, *others):
            out = []
            for shift in shifts:
                part = lax.dynamic_index_in_dim(plain, (tp + shift) % n_tp, 1, keepdims=False)
                out.append(part[:, order[first : first + count]].reshape(rows, count * UNIT))
            return out

    far = list(range(1, n_tp))
    n_far = len(far)
    own_a = restored_units([0], 0, counts[0])[0]
    far_units = restored_units(far, 0, counts[0]) if far else []
    step_masks = range(n_pieces)
    relative = np.zeros((2, n_pieces), np.int32)
    for k in range(2):
        for m in step_masks:
            for s in range(len(bits)):
                if m >> s & 1:
                    relative[k, m] ^= bit_of(s, k)
    relative = jnp.asarray(relative)
    shifts = jnp.arange(n_tp, dtype=jnp.int32)

    def depth_blocks(of_rep):
        source = of_rep ^ relative[of_rep % 2]
        server = (tp - shifts) % n_tp
        return (source[None, :] * n_tp + server[:, None]).reshape(-1)

    table = jnp.concatenate(
        [depth_blocks(r).reshape(n_tp, n_pieces) for r in (rep, rep ^ 1)], axis=0
    )
    pieces = []
    served = {}
    fences = {}
    n_units = 2 + 3 * n_far

    def arrived(u):
        return () if u < 0 else tuple(pieces[u][1:-1]) + (tuple(pieces[u - 1][-1:]) if u > 0 else ())

    def near(u):
        return pieces[u][min(1, n_pieces - 1)]

    def serve(u, held):
        fence = (near(u - 4),) if u >= 4 else ()
        served[u] = to_server(after(held, *fence), far[(u - 2) % n_far])

    def gather(held):
        u = len(pieces)
        got = [after(held, *arrived(u - 2), *fences.get(u, ()))]
        for step in range(len(bits)):
            got += [gather_step(g, step) for g in got]
        pieces.append(got)

    gather(own_a)
    for u in range(2, 2 + min(n_far, 3)):
        serve(u, far_units[u - 2])
    own_b = restored_units([0], counts[0], counts[1] + counts[2])[0]
    gather(own_b)
    far_units += restored_units(far, starts[1], counts[1])
    far_units += restored_units(far, starts[2], counts[2])
    parts = norm(hidden, norm_gain, table, rows)
    tokens = [[to_core(p) for p in parts[n_tp:]], parts[:n_tp]]
    segments = segment_ids[0]
    cosine, sine = rotary_tables(token_positions(segments))
    bias = qkv_bias.astype(jnp.float32).reshape(1, full_width)
    held = key = value = None
    base = 0
    for c in range(3):
        width = counts[c] * UNIT
        offset = (starts[c] - starts[min(c, 1)]) * UNIT
        columns = tp * local_units + jnp.asarray(order[starts[c] : starts[c] + counts[c]])
        for n in range(n_far):
            u = len(pieces)
            if u not in served:
                serve(u, far_units[u - 2])
            gather(served[u])
        chunk = [p for got in pieces[2 + c * n_far :] for p in got]
        both = pieces[min(c, 1)] + chunk
        offsets = [offset] * n_pieces + [0] * len(chunk)
        if c < 2:
            theirs, mine = product(tokens, both, offsets, width)
            other = to_core(theirs)
            if c == 0:
                fences[n_units - 2] = (theirs, mine)
        else:
            cut = len(both) - n_pieces
            partial = product([x[:-1] for x in tokens], both[:cut], offsets[:cut], width)
            last = functools.partial(product, pieces=both[cut:], offsets=offsets[cut:], width=width)
            other = to_core(last([tokens[0][-1:]], accs=partial[:1])[0])
            mine = last([tokens[1][-1:]], accs=partial[1:])[0]
        skip = 0
        if c == 0:
            skip = groups
            key, value = key_value(mine, other, bias, cosine, sine, columns[:groups], dtype)
        held = attention(
            mine, other, bias, cosine, sine, key, value, segments, held,
            columns[skip:], skip, base, groups * (HEADS // KV) * HD,
        )
        base += counts[c] - skip
        if c == 0:
            block_peak = peaks_here(qkv_weight, peaks, shared)
            fences[n_units - 1] = (held,)
            fences[n_units - 2] = fences.get(n_units - 2, ()) + (block_peak,)
    return held, block_peak


def solution(mesh):
    placed = (P("rep", None), P("rep", None), P(), P(("rep", "tp"), None), P())
    return jax.shard_map(
        shards,
        mesh=mesh,
        in_specs=placed,
        out_specs=(P("rep", "tp"), P(None, "tp")),
        check_vma=False,
    )
```
